256 devices in a mesh: row: 16 (over x, y), col: 16 (over z, core).
Axes of the slice: x: 4, y: 4, z: 8, core: 2. Of those that a mesh axis runs over, the one named last changes fastest.
Arguments:
- tile_values: bfloat16 [16, 256, 512, 512], P('row', 'col'), may hold values from -0.0625 to 0.0625
- tile_rows: int32 [16, 256], P('row', 'col'), may hold values from 0 to 15, as said below
- tile_cols: int32 [16, 256], P('row', 'col'), may hold values from 0 to 15
- tile_count: int32 [16, 16], P('row', 'col'), may hold values from 1 to 16, as said below
- start_block: float32 [64, 131072], P(None, ('row', 'col')), may hold values from -6 to 6
Outputs:
- lanczos_basis: float32 [3, 64, 131072], P(None, None, ('row', 'col'))
- recurrence: float32 [3, 2, 64, 64], replicated
The draws below stay inside these ranges and needn't reach their ends.
Inputs may be any that keep to these rules, and one draw needn't show every extreme that they name: For s < tile_count the pairs (tile_rows, tile_cols) of one grid position are distinct and give I <= J; later slots hold indices in range that are not used. `tile_count`: grid position (0, 0) uses all 16 slots.
All inputs are finite; a program needn't handle non-finite values.
Results may differ from the reference program's by a relative error of at most 0.0044.
Values may be sent and summed in bfloat16 or wider, within the bound.
No kernel may reach another device: no remote copies, remote signals or barrier semaphores. Data moves between devices by JAX's collectives and lax.ppermute only.
A program may use at most 64 MiB of HBM per device.

```python
import jax
import jax.numpy as jnp
from jax import lax

BS = 512
K = 64
VB = 1
CAP = 16
ITERS = 3
NLAB = 131072
N_ROW = 16
N_COL = 16


def tile_layout(key):
    local_rows = N_COL * VB
    local_cols = N_ROW * VB
    candidates = local_rows * local_cols
    grid_row = jnp.arange(N_ROW, dtype=jnp.int32)[:, None, None]
    grid_col = jnp.arange(N_COL, dtype=jnp.int32)[None, :, None]
    slot_ids = jnp.arange(candidates, dtype=jnp.int32)[None, None, :]
    cand_rows = slot_ids // local_cols
    cand_cols = slot_ids % local_cols
    block_row = (grid_row * N_COL + cand_rows // VB) * VB + cand_rows % VB
    block_col = (cand_cols // VB * N_COL + grid_col) * VB + cand_cols % VB
    upper_ok = block_row <= block_col
    first_key, second_key = jax.random.split(key)
    scores = jax.random.randint(first_key, (N_ROW, N_COL, candidates), 0, 1024) * candidates + slot_ids
    scores = scores + jnp.where(upper_ok, 0, 2048 * candidates)
    ranked = jnp.argsort(scores, axis=-1, stable=True)[:, :, :CAP]
    shape_all = (N_ROW, N_COL, candidates)
    picked_rows = jnp.take_along_axis(jnp.broadcast_to(cand_rows, shape_all), ranked, axis=-1)
    picked_cols = jnp.take_along_axis(jnp.broadcast_to(cand_cols, shape_all), ranked, axis=-1)
    upper_total = jnp.sum(upper_ok.astype(jnp.int32), axis=-1)
    wanted = jax.random.randint(second_key, (N_ROW, N_COL), max(1, CAP // 4), CAP + 1)
    counts = jnp.minimum(wanted, upper_total)
    counts = counts.at[0, 0].set(CAP)
    return (picked_rows.reshape(N_ROW, N_COL * CAP).astype(jnp.int32), picked_cols.reshape(N_ROW, N_COL * CAP).astype(jnp.int32), counts.astype(jnp.int32))


def draw_tile_rows(key, part):
    return tile_layout(key)[0]


def draw_tile_cols(key, part):
    return tile_layout(key)[1]


def draw_tile_count(key, part):
    return tile_layout(key)[2]


def levels(key, shape, pieces, smallest, top_value):
    loudness, own = 1.0, jax.random.fold_in(key, 6)
    for position, parts in pieces:
        heights = jnp.exp(jax.random.uniform(jax.random.fold_in(own, position), (parts,), jnp.float32, smallest / len(pieces), top_value / len(pieces)))
        loudness = loudness * jnp.repeat(heights, shape[position] // parts).reshape([-1 if axis == position else 1 for axis in range(len(shape))])
    return loudness


def bell_draw(own_key, dims, spread, reach, cuts=(), kind=jnp.bfloat16):
    factor_of = levels(own_key, dims, cuts, -0.22, 0.18) if cuts else 1.0
    drawn = jax.random.normal(own_key, dims, jnp.float32) * spread * factor_of
    return jnp.minimum(jnp.maximum(drawn, -reach), reach).astype(kind)


def setup_inputs(seed: int = 0) -> dict:
    seeds = jax.random.split(jax.random.key(seed), 6)
    return {
        "tile_values": bell_draw(seeds[0], (N_ROW, N_COL * CAP, BS, BS), (CAP * BS) ** -0.5, 0.0625, ((0, 16), (1, 16))),
        "tile_rows": draw_tile_rows(jax.random.fold_in(seeds[5], 71), 0),
        "tile_cols": draw_tile_cols(jax.random.fold_in(seeds[5], 71), 0),
        "tile_count": draw_tile_count(jax.random.fold_in(seeds[5], 71), 0),
        "start_block": bell_draw(seeds[4], (K, NLAB), 1.0, 6.0, ((1, 256),), jnp.float32),
    }


def block_coords(tile_rows, tile_cols):
    slot_rows = tile_rows.reshape(N_ROW, N_COL, CAP).astype(jnp.int32)
    slot_cols = tile_cols.reshape(N_ROW, N_COL, CAP).astype(jnp.int32)
    grid_row = jnp.arange(N_ROW, dtype=jnp.int32)[:, None, None]
    grid_col = jnp.arange(N_COL, dtype=jnp.int32)[None, :, None]
    block_row = (grid_row * N_COL + slot_rows // VB) * VB + slot_rows % VB
    block_col = (slot_cols // VB * N_COL + grid_col) * VB + slot_cols % VB
    return (block_row.reshape(-1), block_col.reshape(-1))

def apply_operator(vectors, flat_tiles, block_row, block_col, in_use):

    def visit(totals, element):
        this_tile, row_index, col_index, active = element

        def accumulate(totals):
            row_start = (row_index * BS).astype(jnp.int32)
            col_start = (col_index * BS).astype(jnp.int32)
            col_vectors = lax.dynamic_slice_in_dim(vectors, col_start, BS, 1)
            row_vectors = lax.dynamic_slice_in_dim(vectors, row_start, BS, 1)
            forward_term = lax.dot_general(col_vectors.astype(jnp.float32), this_tile.astype(jnp.float32), (((1,), (1,)), ((), ())), preferred_element_type=jnp.float32)
            backward_term = jnp.dot(row_vectors.astype(jnp.float32), this_tile.astype(jnp.float32), preferred_element_type=jnp.float32)
            totals = lax.dynamic_update_slice_in_dim(totals, lax.dynamic_slice_in_dim(totals, row_start, BS, 1) + forward_term, row_start, 1)
            totals = lax.dynamic_update_slice_in_dim(totals, lax.dynamic_slice_in_dim(totals, col_start, BS, 1) + backward_term, col_start, 1)
            return totals

        def unchanged(totals):
            return totals
        return (lax.cond(active, accumulate, unchanged, totals), None)
    initial = jnp.zeros((K, NLAB), jnp.float32)
    totals, _ = lax.scan(visit, initial, (flat_tiles, block_row, block_col, in_use))
    return totals

def inner(left, right):
    return jnp.dot(left, right.T, precision=lax.Precision.HIGHEST) / NLAB

def orthonormal(block):
    lower_factor = jnp.linalg.cholesky(inner(block, block))
    return (jax.scipy.linalg.solve_triangular(lower_factor, block, lower=True), lower_factor)

def reference(tile_values, tile_rows, tile_cols, tile_count, start_block):
    flat_tiles = tile_values.reshape(N_ROW * N_COL * CAP, BS, BS)
    block_row, block_col = block_coords(tile_rows, tile_cols)
    in_use = (jnp.arange(CAP, dtype=jnp.int32)[None, None, :] < tile_count[:, :, None]).reshape(-1)
    current, _ = orthonormal(start_block)
    basis_list = [current]
    records = []
    for iteration in range(ITERS):
        vectors = basis_list[-1].astype(jnp.bfloat16)
        product = apply_operator(vectors, flat_tiles, block_row, block_col, in_use)
        coeffs = jnp.stack([inner(earlier, product) for earlier in basis_list])
        residual = product
        for index in range(len(basis_list)):
            residual = residual - jnp.dot(coeffs[index].T, basis_list[index], precision=lax.Precision.HIGHEST)
        current, lower_factor = orthonormal(residual)
        records.append(jnp.stack([coeffs[iteration], lower_factor.T]))
        basis_list.append(current)
    return (jnp.stack(basis_list[1:]), jnp.stack(records))
```

```python
import functools

import jax
import jax.numpy as jnp
from jax import lax
from jax.experimental import pallas as pl
from jax.experimental.pallas import tpu as pltpu
from jax.sharding import PartitionSpec as P

ITERS = 3
K = 64
BS = 512
N_ROW = 16
N_COL = 16
N_Z = 8
CAP = 16
HI = lax.Precision.HIGHEST
VMEM = pl.BlockSpec(memory_space=pltpu.VMEM)
PARAMS = pltpu.CompilerParams(vmem_limit_bytes=40 * 1024 * 1024)
F32 = jnp.float32
BF16 = jnp.bfloat16


def dot_nt(left, right):
    return lax.dot_general(left, right, (((1,), (1,)), ((), ())), precision=HI, preferred_element_type=F32)


def dot_nn(left, right):
    return lax.dot_general(left, right, (((1,), (0,)), ((), ())), precision=HI, preferred_element_type=F32)


def permute(x, axis, pairs):
    return lax.ppermute(x, axis, pairs)


def xor_pairs(n, mask):
    return [(i, i ^ mask) for i in range(n)]


def z_pairs(shift):
    return [(2 * z + core, 2 * ((z + shift) % N_Z) + core) for z in range(N_Z) for core in range(2)]


def exchange_sum(x, axis, n, unit):
    p1 = permute(x, axis, xor_pairs(n, unit))
    p2 = permute(x, axis, xor_pairs(n, 2 * unit))
    p3 = permute(x, axis, xor_pairs(n, 3 * unit))
    return (x + p1) + (p2 + p3)


def all_sum(x):
    x = exchange_sum(x, "col", N_COL, 1)
    x = exchange_sum(x, "row", N_ROW, 1)
    x = exchange_sum(x, "row", N_ROW, 4)
    return exchange_sum(x, "col", N_COL, 4)


def forward_kernel(rows, cols, meta, tile, vecs, mine, other, acc):
    step = pl.program_id(0)
    core, z = meta[1], meta[2]

    @pl.when(step == 0)
    def _():
        acc[...] = jnp.zeros_like(acc)

    @pl.when(step < meta[0])
    def _():
        a = rows[step]
        acc[a] += lax.dot_general(
            vecs[cols[step]], tile[0], (((1,), (1,)), ((), ())), preferred_element_type=F32
        )

    @pl.when(step == CAP - 1)
    def _():
        for shift in range(N_Z):
            target = lax.rem(z + shift, N_Z)
            mine[shift] = acc[2 * target + core]
            other[shift] = acc[2 * target + 1 - core]


def backward_kernel(rows, cols, meta, tile, own, twin, out, acc):
    step = pl.program_id(0)
    core, z = meta[1], meta[2]

    @pl.when(step == 0)
    def _():
        acc[...] = jnp.zeros_like(acc)

    @pl.when(step < meta[0])
    def _():
        a = rows[step]
        shift = lax.rem(z + N_Z - a // 2, N_Z)
        local = lax.rem(a, 2) == core
        piece = jnp.where(local, own[shift], twin[shift])
        acc[cols[step]] += lax.dot_general(
            piece, tile[0], (((1,), (0,)), ((), ())), preferred_element_type=F32
        )

    @pl.when(step == CAP - 1)
    def _():
        out[...] = acc[...].astype(BF16)


def tile_call(kernel, tiles, rows, cols, meta, vectors, out_shape):
    whole = lambda shape: pl.BlockSpec(shape, lambda s, r, c, m: (0,) * len(shape))
    tile_spec = pl.BlockSpec((1, BS, BS), lambda s, r, c, m: (jnp.minimum(s, m[0] - 1), 0, 0))
    return pl.pallas_call(
        kernel,
        out_shape=out_shape,
        grid_spec=pltpu.PrefetchScalarGridSpec(
            num_scalar_prefetch=3,
            grid=(CAP,),
            in_specs=[tile_spec] + [whole(v.shape) for v in vectors],
            out_specs=jax.tree.map(lambda o: whole(o.shape), out_shape),
            scratch_shapes=[pltpu.VMEM((16, K, BS), F32)],
        ),
        compiler_params=PARAMS,
    )(rows, cols, meta, tiles, *vectors)


def join_kernel(mine, other, *outs):
    for shift in range(N_Z):
        outs[shift][...] = (mine[shift] + other[shift]).astype(BF16)


def join(mine, other):
    shape = jax.ShapeDtypeStruct((K, BS), BF16)
    return pl.pallas_call(
        join_kernel,
        out_shape=[shape] * N_Z,
        in_specs=[VMEM] * 2,
        out_specs=[VMEM] * N_Z,
        compiler_params=PARAMS,
    )(mine, other)


def product_kernel(n_basis, by_row, *refs):
    pieces = refs[:N_Z]
    basis = refs[N_Z : N_Z + n_basis]
    product_ref, inner_ref = refs[N_Z + n_basis :]
    total = by_row[0].astype(F32)
    for i in range(1, N_ROW):
        total = total + by_row[i].astype(F32)
    for piece in pieces:
        total = total + piece[...].astype(F32)
    product_ref[...] = total
    for i in range(n_basis):
        inner_ref[:, i * K : (i + 1) * K] = dot_nt(total, basis[i][...])
    inner_ref[:, n_basis * K : (n_basis + 1) * K] = dot_nt(total, total)


def product_call(by_row, pieces, basis):
    n = len(basis)
    return pl.pallas_call(
        functools.partial(product_kernel, n),
        out_shape=[
            jax.ShapeDtypeStruct((K, BS), F32),
            jax.ShapeDtypeStruct((K, (n + 1) * K), F32),
        ],
        in_specs=[VMEM] * (1 + N_Z + n),
        out_specs=[VMEM] * 2,
        compiler_params=PARAMS,
    )(by_row, *pieces, *basis)


def gram_kernel(block, out):
    out[...] = dot_nt(block[...], block[...])


def gram_call(block):
    return pl.pallas_call(
        gram_kernel,
        out_shape=jax.ShapeDtypeStruct((K, K), F32),
        in_specs=[VMEM],
        out_specs=VMEM,
        compiler_params=PARAMS,
    )(block)


def factor(gram):
    row_id = lax.broadcasted_iota(jnp.int32, (K, K), 0)
    col_id = lax.broadcasted_iota(jnp.int32, (K, K), 1)
    unit = (row_id == col_id).astype(F32)
    work = jnp.concatenate([gram, unit], axis=1)
    ids = lax.broadcasted_iota(jnp.int32, (K, 1), 0)
    parts = [work[8 * i : 8 * i + 8] for i in range(K // 8)]
    roots = []
    for k in range(K):
        p, o = divmod(k, 8)
        pivot_row = parts[p][o : o + 1]
        pivot = pivot_row[:, k : k + 1]
        roots.append(pivot)
        if k == K - 1:
            break
        scaled = pivot_row / pivot
        first = p if o < 7 else p + 1
        for i in range(first, K // 8):
            column = parts[i][:, k : k + 1]
            if i == p:
                column = jnp.where(ids[8 * i : 8 * i + 8] > k, column, 0.0)
            parts[i] = parts[i] - column * scaled
    work = jnp.concatenate(parts, axis=0)
    scale = jnp.concatenate(roots, axis=0)
    work = work / jnp.sqrt(scale)
    upper = jnp.where(row_id <= col_id, work[:, :K], 0.0)
    inverse = jnp.where(row_id >= col_id, work[:, K:], 0.0)
    return upper, inverse


def finish_kernel(n_basis, labels, send, sums, block_ref, *refs):
    basis = refs[:n_basis]
    outs = refs[n_basis:]
    current_ref, record_ref = outs[:2]
    inner = sums[...] / labels
    gram = inner[:, n_basis * K : (n_basis + 1) * K]
    residual = block_ref[...]
    for i in range(n_basis):
        coeffs_t = inner[:, i * K : (i + 1) * K]
        gram = gram - dot_nt(coeffs_t, coeffs_t)
        residual = residual - dot_nn(coeffs_t, basis[i][...])
    upper, inverse = factor(gram)
    current = dot_nn(inverse, residual)
    current_ref[...] = current
    if n_basis:
        record_ref[0] = inner[:, (n_basis - 1) * K : n_basis * K].T
    else:
        record_ref[0] = upper
    record_ref[1] = upper
    if send:
        vectors = current.astype(BF16)
        outs[2][...] = vectors
        for i in range(N_ROW):
            outs[3][i] = vectors


def finish_call(sums, block, basis, labels, send):
    n = len(basis)
    out_shape = [jax.ShapeDtypeStruct((K, BS), F32), jax.ShapeDtypeStruct((2, K, K), F32)]
    if send:
        out_shape += [
            jax.ShapeDtypeStruct((K, BS), BF16),
            jax.ShapeDtypeStruct((N_ROW, K, BS), BF16),
        ]
    return pl.pallas_call(
        functools.partial(finish_kernel, n, labels, send),
        out_shape=out_shape,
        in_specs=[VMEM] * (2 + n),
        out_specs=[VMEM] * len(out_shape),
        compiler_params=PARAMS,
    )(sums, block, *basis)


def per_device(tile_values, tile_rows, tile_cols, tile_count, start_block):
    tiles = tile_values[0]
    rows, cols = tile_rows[0], tile_cols[0]
    place = lax.axis_index("col")
    meta = jnp.stack([tile_count[0, 0], place % 2, place // 2]).astype(jnp.int32)
    labels = float(BS * N_ROW * N_COL)

    sums = all_sum(gram_call(start_block))
    current, _, vectors, spread = finish_call(sums, start_block, [], labels, True)
    basis = [current]
    records = []
    for iteration in range(ITERS):
        col_vectors = lax.all_to_all(spread, "row", 0, 0, tiled=True)
        own = [vectors] + [permute(vectors, "col", z_pairs(s)) for s in range(1, N_Z)]
        own = jnp.stack(own)
        twin = permute(own, "col", xor_pairs(N_COL, 1))
        half = jax.ShapeDtypeStruct((N_Z, K, BS), F32)
        mine, other = tile_call(forward_kernel, tiles, rows, cols, meta, [col_vectors], [half, half])
        other = permute(other, "col", xor_pairs(N_COL, 1))
        part_col = tile_call(
            backward_kernel, tiles, rows, cols, meta, [own, twin],
            jax.ShapeDtypeStruct((N_ROW, K, BS), BF16),
        )
        by_row = lax.all_to_all(part_col, "row", 0, 0, tiled=True)
        pieces = join(mine, other)
        pieces = [pieces[0]] + [permute(pieces[s], "col", z_pairs(s)) for s in range(1, N_Z)]
        product, inner = product_call(by_row, pieces, basis)
        sums = all_sum(inner)
        last = iteration == ITERS - 1
        result = finish_call(sums, product, basis, labels, not last)
        basis.append(result[0])
        records.append(result[1])
        if not last:
            vectors, spread = result[2:]
    return (jnp.stack(basis[1:]), jnp.stack(records))


def solution(mesh):
    in_specs = (
        P("row", "col", None, None),
        P("row", "col"),
        P("row", "col"),
        P("row", "col"),
        P(None, ("row", "col")),
    )
    out_specs = (P(None, None, ("row", "col")), P())
    return jax.shard_map(
        per_device, mesh=mesh, in_specs=in_specs, out_specs=out_specs, check_vma=False
    )
```

```python
import functools

import jax
import jax.numpy as jnp
from jax import lax
from jax.experimental import pallas as pl
from jax.experimental.pallas import tpu as pltpu
from jax.sharding import PartitionSpec as P

ITERS = 3
K = 64
BS = 512
N_ROW = 16
N_COL = 16
N_Z = 8
ROW = ("x", "y")
COL = ("z", "core")
CAP = 16
AHEAD = 3
HI = lax.Precision.HIGHEST
VMEM = pl.BlockSpec(memory_space=pltpu.VMEM)
PARAMS = pltpu.CompilerParams(vmem_limit_bytes=40 * 1024 * 1024)
TILE_PARAMS = pltpu.CompilerParams(vmem_limit_bytes=58 * 1024 * 1024)
F32 = jnp.float32
BF16 = jnp.bfloat16


def dot_nt(left, right):
    return lax.dot_general(left, right, (((1,), (1,)), ((), ())), precision=HI, preferred_element_type=F32)


def dot_nn(left, right):
    return lax.dot_general(left, right, (((1,), (0,)), ((), ())), precision=HI, preferred_element_type=F32)


def permute(x, axis, pairs):
    return lax.ppermute(x, axis, pairs)


TWIN = [(0, 1), (1, 0)]


def z_pairs(shift):
    return [(z, (z + shift) % N_Z) for z in range(N_Z)]


def turn(n, unit, shift):
    return [(i, i - i // unit % 4 * unit + (i // unit + shift) % 4 * unit) for i in range(n)]


def exchange_sum(x, axis, n, unit):
    p1 = permute(x, axis, turn(n, unit, 1))
    p2 = permute(x, axis, turn(n, unit, 2))
    p3 = permute(x, axis, turn(n, unit, 3))
    return (x + p2) + (p1 + p3)


def all_sum(x):
    x = exchange_sum(x, COL, N_COL, 1)
    x = exchange_sum(x, ROW, N_ROW, 1)
    x = exchange_sum(x, ROW, N_ROW, 4)
    return exchange_sum(x, COL, N_COL, 4)


def tile_copies(tiles, store, sems, count):
    for slot in range(CAP):

        @pl.when(slot < count)
        def _():
            pltpu.make_async_copy(tiles.at[slot], store.at[slot], sems.at[slot]).start()


def forward_kernel(rows, cols, meta, tiles, vecs, mine, other, acc, store, sems):
    count, core, z = meta[0], meta[1], meta[2]
    tile_copies(tiles, store, sems, count)
    acc[...] = jnp.zeros_like(acc)

    @pl.loop(0, count)
    def _(slot):
        pltpu.make_async_copy(tiles.at[slot], store.at[slot], sems.at[slot]).wait()
        acc[rows[slot]] += lax.dot_general(
            vecs[cols[slot]], store[slot], (((1,), (1,)), ((), ())), preferred_element_type=F32
        )

    for shift in range(N_Z):
        target = lax.rem(z + shift, N_Z)
        mine[shift] = acc[2 * target + core]
        other[shift] = acc[2 * target + 1 - core]


def backward_kernel(rows, cols, meta, tiles, own, twin, out, acc, store, sems):
    count, core, z = meta[0], meta[1], meta[2]
    tile_copies(tiles, store, sems, count)
    acc[...] = jnp.zeros_like(acc)

    @pl.loop(0, count)
    def _(slot):
        pltpu.make_async_copy(tiles.at[slot], store.at[slot], sems.at[slot]).wait()
        a = rows[slot]
        shift = lax.rem(z + N_Z - a // 2, N_Z)
        local = lax.rem(a, 2) == core
        piece = jnp.where(local, own[shift], twin[shift])
        acc[cols[slot]] += lax.dot_general(
            piece, store[slot], (((1,), (0,)), ((), ())), preferred_element_type=F32
        )

    out[...] = acc[...].astype(BF16)


def tile_call(kernel, tiles, rows, cols, meta, vectors, out_shape):
    smem = pl.BlockSpec(memory_space=pltpu.SMEM)
    return pl.pallas_call(
        kernel,
        out_shape=out_shape,
        in_specs=[smem] * 3 + [pl.BlockSpec(memory_space=pl.ANY)] + [VMEM] * len(vectors),
        out_specs=jax.tree.map(lambda o: VMEM, out_shape),
        scratch_shapes=[
            pltpu.VMEM((16, K, BS), F32),
            pltpu.VMEM((CAP, BS, BS), BF16),
            pltpu.SemaphoreType.DMA((CAP,)),
        ],
        compiler_params=TILE_PARAMS,
    )(rows, cols, meta, tiles, *vectors)


def cast_kernel(block, out):
    out[...] = block[...].astype(BF16)


def cast(block):
    return pl.pallas_call(
        cast_kernel,
        out_shape=jax.ShapeDtypeStruct((K, BS), BF16),
        in_specs=[VMEM],
        out_specs=VMEM,
        compiler_params=PARAMS,
    )(block)


def collect_kernel(*refs):
    for i in range(N_Z):
        refs[N_Z][i] = refs[i][...]


def collect(pieces):
    return pl.pallas_call(
        collect_kernel,
        out_shape=jax.ShapeDtypeStruct((N_Z, K, BS), BF16),
        in_specs=[VMEM] * N_Z,
        out_specs=VMEM,
        compiler_params=PARAMS,
    )(*pieces)


def join_kernel(mine, other, *outs):
    for shift in range(N_Z):
        outs[shift][...] = (mine[shift] + other[shift]).astype(BF16)


def join(mine, other):
    shape = jax.ShapeDtypeStruct((K, BS), BF16)
    return pl.pallas_call(
        join_kernel,
        out_shape=[shape] * N_Z,
        in_specs=[VMEM] * 2,
        out_specs=[VMEM] * N_Z,
        compiler_params=PARAMS,
    )(mine, other)


def product_kernel(n_basis, by_row, *refs):
    pieces = refs[:N_Z]
    basis = refs[N_Z : N_Z + n_basis]
    product_ref, inner_ref = refs[N_Z + n_basis :]
    total = by_row[0].astype(F32)
    for i in range(1, N_ROW):
        total = total + by_row[i].astype(F32)
    for piece in pieces:
        total = total + piece[...].astype(F32)
    product_ref[...] = total
    for i in range(n_basis):
        inner_ref[:, i * K : (i + 1) * K] = dot_nt(total, basis[i][...])
    inner_ref[:, n_basis * K : (n_basis + 1) * K] = dot_nt(total, total)


def product_call(by_row, pieces, basis):
    n = len(basis)
    return pl.pallas_call(
        functools.partial(product_kernel, n),
        out_shape=[
            jax.ShapeDtypeStruct((K, BS), F32),
            jax.ShapeDtypeStruct((K, (n + 1) * K), F32),
        ],
        in_specs=[VMEM] * (1 + N_Z + n),
        out_specs=[VMEM] * 2,
        compiler_params=PARAMS,
    )(by_row, *pieces, *basis)


def gram_kernel(block, out):
    out[...] = dot_nt(block[...], block[...])


def gram_call(block):
    return pl.pallas_call(
        gram_kernel,
        out_shape=jax.ShapeDtypeStruct((K, K), F32),
        in_specs=[VMEM],
        out_specs=VMEM,
        compiler_params=PARAMS,
    )(block)


def factor(gram):
    row_id = lax.broadcasted_iota(jnp.int32, (K, K), 0)
    col_id = lax.broadcasted_iota(jnp.int32, (K, K), 1)
    unit = (row_id == col_id).astype(F32)
    work = jnp.concatenate([gram, unit], axis=1)
    ids = lax.broadcasted_iota(jnp.int32, (8, 1), 0)
    n = K // 8
    parts = [work[8 * i : 8 * i + 8] for i in range(n)]
    columns = {}

    def take(c):
        columns[c] = {
            i: jnp.broadcast_to(parts[i][:, c : c + 1], (8, 2 * K)) for i in range(c // 8, n)
        }

    for c in range(AHEAD):
        take(c)
    for k in range(K - 1):
        p, o = divmod(k, 8)
        if k + AHEAD < K:
            take(k + AHEAD)
        column = columns.pop(k)
        inverse = 1.0 / column[p][o : o + 1]
        scaled = parts[p][o : o + 1] * inverse
        for c in range(k + 1, min(k + AHEAD + 1, K)):
            q, r = divmod(c, 8)
            factor_c = column[q][r : r + 1] * inverse
            for i in range(q, n):
                columns[c][i] = columns[c][i] - column[i] * factor_c
        for i in range(p, n):
            multiplier = jnp.where(ids > o, column[i], 0.0) if i == p else column[i]
            parts[i] = parts[i] - multiplier * scaled
    work = jnp.concatenate(parts, axis=0)
    scale = jnp.sum(jnp.where(row_id == col_id, work[:, :K], 0.0), axis=1, keepdims=True)
    work = work * (1.0 / jnp.sqrt(scale))
    upper = jnp.where(row_id <= col_id, work[:, :K], 0.0)
    inverse = jnp.where(row_id >= col_id, work[:, K:], 0.0)
    return upper, inverse


def finish_kernel(n_basis, labels, send, sums, block_ref, *refs):
    basis = refs[:n_basis]
    outs = refs[n_basis:]
    current_ref, record_ref = outs[:2]
    inner = sums[...] / labels
    gram = inner[:, n_basis * K : (n_basis + 1) * K]
    residual = block_ref[...]
    for i in range(n_basis):
        coeffs_t = inner[:, i * K : (i + 1) * K]
        gram = gram - dot_nt(coeffs_t, coeffs_t)
        residual = residual - dot_nn(coeffs_t, basis[i][...])
    upper, inverse = factor(gram)
    current = dot_nn(inverse, residual)
    current_ref[...] = current
    if n_basis:
        record_ref[0] = inner[:, (n_basis - 1) * K : n_basis * K].T
    else:
        record_ref[0] = upper
    record_ref[1] = upper
    if send:
        vectors = current.astype(BF16)
        for i in range(N_ROW):
            outs[2][i] = vectors


def finish_call(sums, block, basis, labels, send):
    n = len(basis)
    out_shape = [jax.ShapeDtypeStruct((K, BS), F32), jax.ShapeDtypeStruct((2, K, K), F32)]
    if send:
        out_shape.append(jax.ShapeDtypeStruct((N_ROW, K, BS), BF16))
    return pl.pallas_call(
        functools.partial(finish_kernel, n, labels, send),
        out_shape=out_shape,
        in_specs=[VMEM] * (2 + n),
        out_specs=[VMEM] * len(out_shape),
        compiler_params=PARAMS,
    )(sums, block, *basis)


def per_device(tile_values, tile_rows, tile_cols, tile_count, start_block):
    tiles = tile_values[0]
    rows, cols = tile_rows[0], tile_cols[0]
    place = [lax.axis_index("core"), lax.axis_index("z")]
    meta = jnp.stack([tile_count[0, 0]] + place).astype(jnp.int32)
    labels = float(BS * N_ROW * N_COL)

    sums = all_sum(gram_call(start_block))
    current, _, spread = finish_call(sums, start_block, [], labels, True)
    basis = [current]
    records = []
    for iteration in range(ITERS):
        col_vectors = lax.all_to_all(spread, ROW, 0, 0, tiled=True)
        vectors = cast(basis[-1])
        own = collect([vectors] + [permute(vectors, "z", z_pairs(s)) for s in range(1, N_Z)])
        twin = permute(own, "core", TWIN)
        half = jax.ShapeDtypeStruct((N_Z, K, BS), F32)
        mine, other = tile_call(forward_kernel, tiles, rows, cols, meta, [col_vectors], [half, half])
        other = permute(other, "core", TWIN)
        part_col = tile_call(
            backward_kernel, tiles, rows, cols, meta, [own, twin],
            jax.ShapeDtypeStruct((N_ROW, K, BS), BF16),
        )
        by_row = lax.all_to_all(part_col, ROW, 0, 0, tiled=True)
        pieces = join(mine, other)
        pieces = [pieces[0]] + [permute(pieces[s], "z", z_pairs(s)) for s in range(1, N_Z)]
        product, inner = product_call(by_row, pieces, basis)
        sums = all_sum(inner)
        last = iteration == ITERS - 1
        result = finish_call(sums, product, basis, labels, not last)
        basis.append(result[0])
        records.append(result[1])
        if not last:
            spread = result[2]
    return (jnp.stack(basis[1:]), jnp.stack(records))


def solution(mesh):
    devices = mesh.devices.reshape(4, 4, N_Z, 2)
    fine = jax.sharding.Mesh(devices, ROW + COL)
    in_specs = (
        P(ROW, COL, None, None),
        P(ROW, COL),
        P(ROW, COL),
        P(ROW, COL),
        P(None, ROW + COL),
    )
    out_specs = (P(None, None, ROW + COL), P())
    return jax.shard_map(
        per_device, mesh=fine, in_specs=in_specs, out_specs=out_specs, check_vma=False
    )
```

```python
import functools

import jax
import jax.numpy as jnp
from jax import lax
from jax.experimental import pallas as pl
from jax.experimental.pallas import tpu as pltpu
from jax.sharding import PartitionSpec as P

ITERS = 3
K = 64
BS = 512
N_ROW = 16
N_COL = 16
N_Z = 8
ROW = ("x", "y")
COL = ("z", "core")
CAP = 16
AHEAD = 3
HI = lax.Precision.HIGHEST
VMEM = pl.BlockSpec(memory_space=pltpu.VMEM)
SMEM = pl.BlockSpec(memory_space=pltpu.SMEM)
PARAMS = pltpu.CompilerParams(vmem_limit_bytes=24 * 1024 * 1024)
F32 = jnp.float32
BF16 = jnp.bfloat16


def dot_nt(left, right):
    return lax.dot_general(left, right, (((1,), (1,)), ((), ())), precision=HI, preferred_element_type=F32)


def dot_nn(left, right):
    return lax.dot_general(left, right, (((1,), (0,)), ((), ())), precision=HI, preferred_element_type=F32)


def permute(x, axis, pairs):
    return lax.ppermute(x, axis, pairs)


TWIN = [(0, 1), (1, 0)]


def z_pairs(shift):
    return [(z, (z + shift) % N_Z) for z in range(N_Z)]


def turn(n, unit, shift):
    return [(i, i - i // unit % 4 * unit + (i // unit + shift) % 4 * unit) for i in range(n)]


def exchange_sum(x, axis, n, unit):
    p1 = permute(x, axis, turn(n, unit, 1))
    p2 = permute(x, axis, turn(n, unit, 2))
    p3 = permute(x, axis, turn(n, unit, 3))
    return (x + p2) + (p1 + p3)


def near_sum(x):
    p1, p2, p3 = [permute(x, COL, [(i, i ^ m) for i in range(N_COL)]) for m in (1, 2, 3)]
    return (x + p1) + (p2 + p3)


def all_sum(x):
    x = near_sum(x)
    x = exchange_sum(x, ROW, N_ROW, 1)
    x = exchange_sum(x, ROW, N_ROW, 4)
    return exchange_sum(x, COL, N_COL, 4)


def forward_kernel(rows, cols, meta, tiles, vecs, mine, other, acc):
    core, z = meta[1], meta[2]
    acc[...] = jnp.zeros_like(acc)

    @pl.loop(0, meta[0])
    def _(slot):
        acc[rows[slot]] += lax.dot_general(
            vecs[cols[slot]], tiles[slot], (((1,), (1,)), ((), ())), preferred_element_type=F32
        )

    for shift in range(N_Z):
        target = lax.rem(z + shift, N_Z)
        mine[shift] = acc[2 * target + core]
        other[shift] = acc[2 * target + 1 - core]


def backward_kernel(rows, cols, meta, tiles, own, twin, out, acc):
    core, z = meta[1], meta[2]
    acc[...] = jnp.zeros_like(acc)

    @pl.loop(0, meta[0])
    def _(slot):
        a = rows[slot]
        shift = lax.rem(z + N_Z - a // 2, N_Z)
        local = lax.rem(a, 2) == core
        piece = jnp.where(local, own[shift], twin[shift])
        acc[cols[slot]] += lax.dot_general(
            piece, tiles[slot], (((1,), (0,)), ((), ())), preferred_element_type=F32
        )

    out[...] = acc[...].astype(BF16)


def tile_call(kernel, tiles, rows, cols, meta, vectors, out_shape):
    return pl.pallas_call(
        kernel,
        out_shape=out_shape,
        in_specs=[SMEM] * 3 + [VMEM] * (1 + len(vectors)),
        out_specs=jax.tree.map(lambda o: VMEM, out_shape),
        scratch_shapes=[pltpu.VMEM((16, K, BS), F32)],
        compiler_params=PARAMS,
    )(rows, cols, meta, tiles, *vectors)


def cast_kernel(block, out):
    out[...] = block[...].astype(BF16)


def cast(block):
    return pl.pallas_call(
        cast_kernel,
        out_shape=jax.ShapeDtypeStruct((K, BS), BF16),
        in_specs=[VMEM],
        out_specs=VMEM,
        compiler_params=PARAMS,
    )(block)


def collect_kernel(*refs):
    for i in range(N_Z):
        refs[N_Z][i] = refs[i][...]


def collect(pieces):
    return pl.pallas_call(
        collect_kernel,
        out_shape=jax.ShapeDtypeStruct((N_Z, K, BS), BF16),
        in_specs=[VMEM] * N_Z,
        out_specs=VMEM,
        compiler_params=PARAMS,
    )(*pieces)


def join_kernel(mine, other, *outs):
    for shift in range(N_Z):
        outs[shift][...] = (mine[shift] + other[shift]).astype(BF16)


def join(mine, other):
    shape = jax.ShapeDtypeStruct((K, BS), BF16)
    return pl.pallas_call(
        join_kernel,
        out_shape=[shape] * N_Z,
        in_specs=[VMEM] * 2,
        out_specs=[VMEM] * N_Z,
        compiler_params=PARAMS,
    )(mine, other)


def product_kernel(n_basis, by_row, *refs):
    pieces = refs[:N_Z]
    basis = refs[N_Z : N_Z + n_basis]
    product_ref, inner_ref = refs[N_Z + n_basis :]
    total = by_row[0].astype(F32)
    for i in range(1, N_ROW):
        total = total + by_row[i].astype(F32)
    for piece in pieces:
        total = total + piece[...].astype(F32)
    product_ref[...] = total
    for i in range(n_basis):
        inner_ref[:, i * K : (i + 1) * K] = dot_nt(total, basis[i][...])
    inner_ref[:, n_basis * K : (n_basis + 1) * K] = dot_nt(total, total)


def product_call(by_row, pieces, basis):
    n = len(basis)
    return pl.pallas_call(
        functools.partial(product_kernel, n),
        out_shape=[
            jax.ShapeDtypeStruct((K, BS), F32),
            jax.ShapeDtypeStruct((K, (n + 1) * K), F32),
        ],
        in_specs=[VMEM] * (1 + N_Z + n),
        out_specs=[VMEM] * 2,
        compiler_params=PARAMS,
    )(by_row, *pieces, *basis)


def gram_kernel(block, out):
    out[...] = dot_nt(block[...], block[...])


def gram_call(block):
    return pl.pallas_call(
        gram_kernel,
        out_shape=jax.ShapeDtypeStruct((K, K), F32),
        in_specs=[VMEM],
        out_specs=VMEM,
        compiler_params=PARAMS,
    )(block)


def factor(gram):
    row_id = lax.broadcasted_iota(jnp.int32, (K, K), 0)
    col_id = lax.broadcasted_iota(jnp.int32, (K, K), 1)
    unit = (row_id == col_id).astype(F32)
    work = jnp.concatenate([gram, unit], axis=1)
    ids = lax.broadcasted_iota(jnp.int32, (8, 1), 0)
    n = K // 8
    parts = [work[8 * i : 8 * i + 8] for i in range(n)]
    columns = {}

    def take(c):
        columns[c] = {
            i: jnp.broadcast_to(parts[i][:, c : c + 1], (8, 2 * K)) for i in range(c // 8, n)
        }

    for c in range(AHEAD):
        take(c)
    for k in range(K - 1):
        p, o = divmod(k, 8)
        if k + AHEAD < K:
            take(k + AHEAD)
        column = columns.pop(k)
        inverse = 1.0 / column[p][o : o + 1]
        scaled = parts[p][o : o + 1] * inverse
        for c in range(k + 1, min(k + AHEAD + 1, K)):
            q, r = divmod(c, 8)
            factor_c = column[q][r : r + 1] * inverse
            for i in range(q, n):
                columns[c][i] = columns[c][i] - column[i] * factor_c
        for i in range(p, n):
            multiplier = jnp.where(ids > o, column[i], 0.0) if i == p else column[i]
            parts[i] = parts[i] - multiplier * scaled
    work = jnp.concatenate(parts, axis=0)
    scale = jnp.sum(jnp.where(row_id == col_id, work[:, :K], 0.0), axis=1, keepdims=True)
    work = work * (1.0 / jnp.sqrt(scale))
    upper = jnp.where(row_id <= col_id, work[:, :K], 0.0)
    inverse = jnp.where(row_id >= col_id, work[:, K:], 0.0)
    return upper, inverse


def finish_kernel(n_basis, labels, n_records, sums, block_ref, *refs):
    basis = refs[:n_basis]
    records = refs[n_basis : n_basis + n_records]
    outs = refs[n_basis + n_records :]
    inner = sums[...] / labels
    gram = inner[:, n_basis * K : (n_basis + 1) * K]
    residual = block_ref[...]
    for i in range(n_basis):
        coeffs_t = inner[:, i * K : (i + 1) * K]
        gram = gram - dot_nt(coeffs_t, coeffs_t)
        residual = residual - dot_nn(coeffs_t, basis[i][...])
    upper, inverse = factor(gram)
    current = dot_nn(inverse, residual)
    if n_records:
        basis_ref, record_ref = outs
        for i in range(1, n_basis):
            basis_ref[i - 1] = basis[i][...]
        basis_ref[n_basis - 1] = current
        for i in range(n_records):
            record_ref[i] = records[i][...]
        record_ref[n_records, 0] = inner[:, (n_basis - 1) * K : n_basis * K].T
        record_ref[n_records, 1] = upper
        return
    current_ref, spread_ref = outs[:2]
    current_ref[...] = current
    vectors = current.astype(BF16)
    for i in range(N_ROW):
        spread_ref[i] = vectors
    if n_basis:
        outs[2][0] = inner[:, (n_basis - 1) * K : n_basis * K].T
        outs[2][1] = upper


def finish_call(sums, block, basis, labels, records):
    n = len(basis)
    if records:
        out_shape = [
            jax.ShapeDtypeStruct((n, K, BS), F32),
            jax.ShapeDtypeStruct((n, 2, K, K), F32),
        ]
    else:
        out_shape = [
            jax.ShapeDtypeStruct((K, BS), F32),
            jax.ShapeDtypeStruct((N_ROW, K, BS), BF16),
        ]
        if n:
            out_shape.append(jax.ShapeDtypeStruct((2, K, K), F32))
    return pl.pallas_call(
        functools.partial(finish_kernel, n, labels, len(records)),
        out_shape=out_shape,
        in_specs=[VMEM] * (2 + n + len(records)),
        out_specs=[VMEM] * len(out_shape),
        compiler_params=PARAMS,
    )(sums, block, *basis, *records)


def per_device(tile_values, tile_rows, tile_cols, tile_count, start_block):
    tiles = tile_values[0]
    rows, cols = tile_rows[0], tile_cols[0]
    place = [lax.axis_index("core"), lax.axis_index("z")]
    meta = jnp.stack([tile_count[0, 0]] + place).astype(jnp.int32)
    labels = float(BS * N_ROW * N_COL)

    sums = all_sum(gram_call(start_block))
    current, spread = finish_call(sums, start_block, [], labels, [])
    basis = [current]
    records = []
    for iteration in range(ITERS):
        col_vectors = lax.all_to_all(spread, ROW, 0, 0, tiled=True)
        vectors = cast(basis[-1])
        own = collect([vectors] + [permute(vectors, "z", z_pairs(s)) for s in range(1, N_Z)])
        twin = permute(own, "core", TWIN)
        half = jax.ShapeDtypeStruct((N_Z, K, BS), F32)
        mine, other = tile_call(forward_kernel, tiles, rows, cols, meta, [col_vectors], [half, half])
        other = permute(other, "core", TWIN)
        part_col = tile_call(
            backward_kernel, tiles, rows, cols, meta, [own, twin],
            jax.ShapeDtypeStruct((N_ROW, K, BS), BF16),
        )
        by_row = lax.all_to_all(part_col, ROW, 0, 0, tiled=True)
        pieces = join(mine, other)
        pieces = [pieces[0]] + [permute(pieces[s], "z", z_pairs(s)) for s in range(1, N_Z)]
        product, inner = product_call(by_row, pieces, basis)
        sums = all_sum(inner)
        last = iteration == ITERS - 1
        result = finish_call(sums, product, basis, labels, records if last else [])
        if last:
            return tuple(result)
        current, spread, record = result
        basis.append(current)
        records.append(record)


def solution(mesh):
    devices = mesh.devices.reshape(4, 4, N_Z, 2)
    fine = jax.sharding.Mesh(devices, ROW + COL)
    in_specs = (
        P(ROW, COL, None, None),
        P(ROW, COL),
        P(ROW, COL),
        P(ROW, COL),
        P(None, ROW + COL),
    )
    out_specs = (P(None, None, ROW + COL), P())
    return jax.shard_map(
        per_device, mesh=fine, in_specs=in_specs, out_specs=out_specs, check_vma=False
    )
```

```python
import functools

import jax
import jax.numpy as jnp
from jax import lax
from jax.experimental import pallas as pl
from jax.experimental.pallas import tpu as pltpu
from jax.sharding import PartitionSpec as P

ITERS = 3
K = 64
BS = 512
N_ROW = 16
N_COL = 16
N_Z = 8
N_QUAD = 4
ROW = ("x", "y")
COL = ("z", "core")
CAP = 16
AHEAD = 3
HI = lax.Precision.HIGHEST
VMEM = pl.BlockSpec(memory_space=pltpu.VMEM)
SMEM = pl.BlockSpec(memory_space=pltpu.SMEM)
PARAMS = pltpu.CompilerParams(vmem_limit_bytes=24 * 1024 * 1024)
F32 = jnp.float32
BF16 = jnp.bfloat16


def dot_nt(left, right):
    return lax.dot_general(left, right, (((1,), (1,)), ((), ())), precision=HI, preferred_element_type=F32)


def dot_nn(left, right):
    return lax.dot_general(left, right, (((1,), (0,)), ((), ())), precision=HI, preferred_element_type=F32)


def permute(x, axis, pairs):
    return lax.ppermute(x, axis, pairs)


TWIN = [(0, 1), (1, 0)]


NEXT_Z = [(z, z ^ 1) for z in range(N_Z)]


def z_pairs(step):
    return [(z, (z + 2 * step) % N_Z) for z in range(N_Z)]


def turn(n, unit, shift):
    return [(i, i - i // unit % 4 * unit + (i // unit + shift) % 4 * unit) for i in range(n)]


def exchange_sum(x, axis, n, unit):
    p1 = permute(x, axis, turn(n, unit, 1))
    p2 = permute(x, axis, turn(n, unit, 2))
    p3 = permute(x, axis, turn(n, unit, 3))
    return (x + p2) + (p1 + p3)


def near_sum(x):
    p1, p2, p3 = [permute(x, COL, [(i, i ^ m) for i in range(N_COL)]) for m in (1, 2, 3)]
    return (x + p1) + (p2 + p3)


def all_sum(x):
    x = near_sum(x)
    x = exchange_sum(x, ROW, N_ROW, 1)
    x = exchange_sum(x, ROW, N_ROW, 4)
    return exchange_sum(x, COL, N_COL, 4)


def forward_kernel(rows, cols, meta, tiles, vecs, mine, other, acc):
    core, z = meta[1], meta[2]
    acc[...] = jnp.zeros_like(acc)

    @pl.loop(0, meta[0])
    def _(slot):
        acc[rows[slot]] += lax.dot_general(
            vecs[cols[slot]], tiles[slot], (((1,), (1,)), ((), ())), preferred_element_type=F32
        )

    for i in range(N_Z):
        start = z if i < N_QUAD else z + 1 - 2 * lax.rem(z, 2)
        target = lax.rem(start + 2 * (i % N_QUAD), N_Z)
        mine[i] = acc[2 * target + core]
        other[i] = acc[2 * target + 1 - core]


def backward_kernel(rows, cols, meta, tiles, near, far, near_twin, far_twin, out, acc):
    core, z = meta[1], meta[2]
    acc[...] = jnp.zeros_like(acc)

    @pl.loop(0, meta[0])
    def _(slot):
        a = rows[slot]
        apart = lax.rem(a // 2 + z, 2)
        start = z + apart * (1 - 2 * lax.rem(z, 2))
        step = lax.rem(start + N_Z - a // 2, N_Z) // 2
        here = jnp.where(apart == 0, near[step], far[step])
        there = jnp.where(apart == 0, near_twin[step], far_twin[step])
        piece = jnp.where(lax.rem(a, 2) == core, here, there)
        acc[cols[slot]] += lax.dot_general(
            piece, tiles[slot], (((1,), (0,)), ((), ())), preferred_element_type=F32
        )

    out[...] = acc[...].astype(BF16)


def tile_call(kernel, tiles, rows, cols, meta, vectors, out_shape):
    return pl.pallas_call(
        kernel,
        out_shape=out_shape,
        in_specs=[SMEM] * 3 + [VMEM] * (1 + len(vectors)),
        out_specs=jax.tree.map(lambda o: VMEM, out_shape),
        scratch_shapes=[pltpu.VMEM((16, K, BS), F32)],
        compiler_params=PARAMS,
    )(rows, cols, meta, tiles, *vectors)


def cast_kernel(block, out):
    out[...] = block[...].astype(BF16)


def cast(block):
    return pl.pallas_call(
        cast_kernel,
        out_shape=jax.ShapeDtypeStruct((K, BS), BF16),
        in_specs=[VMEM],
        out_specs=VMEM,
        compiler_params=PARAMS,
    )(block)


def collect_kernel(*refs):
    for i in range(N_QUAD):
        refs[N_QUAD][i] = refs[i][...]


def collect(pieces):
    return pl.pallas_call(
        collect_kernel,
        out_shape=jax.ShapeDtypeStruct((N_QUAD, K, BS), BF16),
        in_specs=[VMEM] * N_QUAD,
        out_specs=VMEM,
        compiler_params=PARAMS,
    )(*pieces)


def pass_kernel(mine, other, out):
    out[...] = (mine[N_QUAD:] + other[N_QUAD:]).astype(BF16)


def pass_on(mine, other):
    return pl.pallas_call(
        pass_kernel,
        out_shape=jax.ShapeDtypeStruct((N_QUAD, K, BS), BF16),
        in_specs=[VMEM] * 2,
        out_specs=VMEM,
        compiler_params=PARAMS,
    )(mine, other)


def join_kernel(mine, other, passed, *outs):
    for i in range(N_QUAD):
        total = mine[i] + other[i] + passed[i].astype(F32)
        outs[i][...] = total.astype(outs[i].dtype)


def join(mine, other, passed):
    return pl.pallas_call(
        join_kernel,
        out_shape=[jax.ShapeDtypeStruct((K, BS), F32)]
        + [jax.ShapeDtypeStruct((K, BS), BF16)] * (N_QUAD - 1),
        in_specs=[VMEM] * 3,
        out_specs=[VMEM] * N_QUAD,
        compiler_params=PARAMS,
    )(mine, other, passed)


def product_kernel(n_basis, by_row, *refs):
    pieces = refs[:N_QUAD]
    basis = refs[N_QUAD : N_QUAD + n_basis]
    product_ref, inner_ref = refs[N_QUAD + n_basis :]
    total = by_row[0].astype(F32)
    for i in range(1, N_ROW):
        total = total + by_row[i].astype(F32)
    for piece in pieces:
        total = total + piece[...].astype(F32)
    product_ref[...] = total
    for i in range(n_basis):
        inner_ref[:, i * K : (i + 1) * K] = dot_nt(total, basis[i][...])
    inner_ref[:, n_basis * K : (n_basis + 1) * K] = dot_nt(total, total)


def product_call(by_row, pieces, basis):
    n = len(basis)
    return pl.pallas_call(
        functools.partial(product_kernel, n),
        out_shape=[
            jax.ShapeDtypeStruct((K, BS), F32),
            jax.ShapeDtypeStruct((K, (n + 1) * K), F32),
        ],
        in_specs=[VMEM] * (1 + N_QUAD + n),
        out_specs=[VMEM] * 2,
        compiler_params=PARAMS,
    )(by_row, *pieces, *basis)


def gram_kernel(block, out):
    out[...] = dot_nt(block[...], block[...])


def gram_call(block):
    return pl.pallas_call(
        gram_kernel,
        out_shape=jax.ShapeDtypeStruct((K, K), F32),
        in_specs=[VMEM],
        out_specs=VMEM,
        compiler_params=PARAMS,
    )(block)


def factor(gram):
    row_id = lax.broadcasted_iota(jnp.int32, (K, K), 0)
    col_id = lax.broadcasted_iota(jnp.int32, (K, K), 1)
    unit = (row_id == col_id).astype(F32)
    work = jnp.concatenate([gram, unit], axis=1)
    ids = lax.broadcasted_iota(jnp.int32, (8, 1), 0)
    n = K // 8
    parts = [work[8 * i : 8 * i + 8] for i in range(n)]
    columns = {}

    def take(c):
        columns[c] = {
            i: jnp.broadcast_to(parts[i][:, c : c + 1], (8, 2 * K)) for i in range(c // 8, n)
        }

    for c in range(AHEAD):
        take(c)
    for k in range(K - 1):
        p, o = divmod(k, 8)
        if k + AHEAD < K:
            take(k + AHEAD)
        column = columns.pop(k)
        inverse = 1.0 / column[p][o : o + 1]
        scaled = parts[p][o : o + 1] * inverse
        for c in range(k + 1, min(k + AHEAD + 1, K)):
            q, r = divmod(c, 8)
            factor_c = column[q][r : r + 1] * inverse
            for i in range(q, n):
                columns[c][i] = columns[c][i] - column[i] * factor_c
        for i in range(p, n):
            multiplier = jnp.where(ids > o, column[i], 0.0) if i == p else column[i]
            parts[i] = parts[i] - multiplier * scaled
    work = jnp.concatenate(parts, axis=0)
    scale = jnp.sum(jnp.where(row_id == col_id, work[:, :K], 0.0), axis=1, keepdims=True)
    work = work * (1.0 / jnp.sqrt(scale))
    upper = jnp.where(row_id <= col_id, work[:, :K], 0.0)
    inverse = jnp.where(row_id >= col_id, work[:, K:], 0.0)
    return upper, inverse


def finish_kernel(n_basis, labels, n_records, sums, block_ref, *refs):
    basis = refs[:n_basis]
    records = refs[n_basis : n_basis + n_records]
    outs = refs[n_basis + n_records :]
    inner = sums[...] / labels
    gram = inner[:, n_basis * K : (n_basis + 1) * K]
    residual = block_ref[...]
    for i in range(n_basis):
        coeffs_t = inner[:, i * K : (i + 1) * K]
        gram = gram - dot_nt(coeffs_t, coeffs_t)
        residual = residual - dot_nn(coeffs_t, basis[i][...])
    upper, inverse = factor(gram)
    current = dot_nn(inverse, residual)
    if n_records:
        basis_ref, record_ref = outs
        for i in range(1, n_basis):
            basis_ref[i - 1] = basis[i][...]
        basis_ref[n_basis - 1] = current
        for i in range(n_records):
            record_ref[i] = records[i][...]
        record_ref[n_records, 0] = inner[:, (n_basis - 1) * K : n_basis * K].T
        record_ref[n_records, 1] = upper
        return
    current_ref, spread_ref = outs[:2]
    current_ref[...] = current
    vectors = current.astype(BF16)
    for i in range(N_ROW):
        spread_ref[i] = vectors
    if n_basis:
        outs[2][0] = inner[:, (n_basis - 1) * K : n_basis * K].T
        outs[2][1] = upper


def finish_call(sums, block, basis, labels, records):
    n = len(basis)
    if records:
        out_shape = [
            jax.ShapeDtypeStruct((n, K, BS), F32),
            jax.ShapeDtypeStruct((n, 2, K, K), F32),
        ]
    else:
        out_shape = [
            jax.ShapeDtypeStruct((K, BS), F32),
            jax.ShapeDtypeStruct((N_ROW, K, BS), BF16),
        ]
        if n:
            out_shape.append(jax.ShapeDtypeStruct((2, K, K), F32))
    return pl.pallas_call(
        functools.partial(finish_kernel, n, labels, len(records)),
        out_shape=out_shape,
        in_specs=[VMEM] * (2 + n + len(records)),
        out_specs=[VMEM] * len(out_shape),
        compiler_params=PARAMS,
    )(sums, block, *basis, *records)


def per_device(tile_values, tile_rows, tile_cols, tile_count, start_block):
    tiles = tile_values[0]
    rows, cols = tile_rows[0], tile_cols[0]
    place = [lax.axis_index("core"), lax.axis_index("z")]
    meta = jnp.stack([tile_count[0, 0]] + place).astype(jnp.int32)
    labels = float(BS * N_ROW * N_COL)

    sums = all_sum(gram_call(start_block))
    current, spread = finish_call(sums, start_block, [], labels, [])
    basis = [current]
    records = []
    for iteration in range(ITERS):
        col_vectors = lax.all_to_all(spread, ROW, 0, 0, tiled=True)
        vectors = cast(basis[-1])
        near = collect([vectors] + [permute(vectors, "z", z_pairs(s)) for s in range(1, N_QUAD)])
        far = permute(near, "z", NEXT_Z)
        near_twin = permute(near, "core", TWIN)
        far_twin = permute(far, "core", TWIN)
        half = jax.ShapeDtypeStruct((N_Z, K, BS), F32)
        mine, other = tile_call(forward_kernel, tiles, rows, cols, meta, [col_vectors], [half, half])
        other = permute(other, "core", TWIN)
        part_col = tile_call(
            backward_kernel, tiles, rows, cols, meta, [near, far, near_twin, far_twin],
            jax.ShapeDtypeStruct((N_ROW, K, BS), BF16),
        )
        by_row = lax.all_to_all(part_col, ROW, 0, 0, tiled=True)
        passed = permute(pass_on(mine, other), "z", NEXT_Z)
        pieces = join(mine, other, passed)
        pieces = [pieces[0]] + [permute(pieces[s], "z", z_pairs(s)) for s in range(1, N_QUAD)]
        product, inner = product_call(by_row, pieces, basis)
        sums = all_sum(inner)
        last = iteration == ITERS - 1
        result = finish_call(sums, product, basis, labels, records if last else [])
        if last:
            return tuple(result)
        current, spread, record = result
        basis.append(current)
        records.append(record)


def solution(mesh):
    devices = mesh.devices.reshape(4, 4, N_Z, 2)
    fine = jax.sharding.Mesh(devices, ROW + COL)
    in_specs = (
        P(ROW, COL, None, None),
        P(ROW, COL),
        P(ROW, COL),
        P(ROW, COL),
        P(None, ROW + COL),
    )
    out_specs = (P(None, None, ROW + COL), P())
    return jax.shard_map(
        per_device, mesh=fine, in_specs=in_specs, out_specs=out_specs, check_vma=False
    )
```

```python
import functools

import jax
import jax.numpy as jnp
from jax import lax
from jax.experimental import pallas as pl
from jax.experimental.pallas import tpu as pltpu
from jax.sharding import PartitionSpec as P

ITERS = 3
K = 64
BS = 512
N_ROW = 16
N_COL = 16
N_Z = 8
N_QUAD = 4
ROW = ("x", "y")
COL = ("z", "core")
CAP = 16
AHEAD = 3
HI = lax.Precision.HIGHEST
VMEM = pl.BlockSpec(memory_space=pltpu.VMEM)
SMEM = pl.BlockSpec(memory_space=pltpu.SMEM)
PARAMS = pltpu.CompilerParams(vmem_limit_bytes=24 * 1024 * 1024)
F32 = jnp.float32
BF16 = jnp.bfloat16


def dot_nt(left, right):
    return lax.dot_general(left, right, (((1,), (1,)), ((), ())), precision=HI, preferred_element_type=F32)


def dot_nn(left, right):
    return lax.dot_general(left, right, (((1,), (0,)), ((), ())), precision=HI, preferred_element_type=F32)


def permute(x, axis, pairs):
    return lax.ppermute(x, axis, pairs)


TWIN = [(0, 1), (1, 0)]


NEXT_Z = [(z, z ^ 1) for z in range(N_Z)]


def z_pairs(step):
    return [(z, (z + 2 * step) % N_Z) for z in range(N_Z)]


def turn(n, unit, shift):
    return [(i, i - i // unit % 4 * unit + (i // unit + shift) % 4 * unit) for i in range(n)]


def exchange_sum(x, axis, n, unit):
    p1 = permute(x, axis, turn(n, unit, 1))
    p2 = permute(x, axis, turn(n, unit, 2))
    p3 = permute(x, axis, turn(n, unit, 3))
    return (x + p2) + (p1 + p3)


def near_sum(x):
    p1, p2, p3 = [permute(x, COL, [(i, i ^ m) for i in range(N_COL)]) for m in (1, 2, 3)]
    return (x + p1) + (p2 + p3)


def all_sum(x):
    x = near_sum(x)
    x = exchange_sum(x, ROW, N_ROW, 1)
    x = exchange_sum(x, ROW, N_ROW, 4)
    return exchange_sum(x, COL, N_COL, 4)


def forward_kernel(rows, cols, meta, tiles, vecs, arrived, mine, other, acc):
    core, z = meta[1], meta[2]
    acc[...] = jnp.zeros_like(acc)

    @pl.loop(0, meta[0])
    def _(slot):
        acc[rows[slot]] += lax.dot_general(
            vecs[cols[slot]], tiles[slot], (((1,), (1,)), ((), ())), preferred_element_type=F32
        )

    for i in range(N_Z):
        start = z if i < N_QUAD else z + 1 - 2 * lax.rem(z, 2)
        target = lax.rem(start + 2 * (i % N_QUAD), N_Z)
        mine[i] = acc[2 * target + core]
        other[i] = acc[2 * target + 1 - core]


def backward_kernel(rows, cols, meta, tiles, near, far, near_twin, far_twin, out, acc):
    core, z = meta[1], meta[2]
    acc[...] = jnp.zeros_like(acc)

    @pl.loop(0, meta[0])
    def _(slot):
        a = rows[slot]
        apart = lax.rem(a // 2 + z, 2)
        start = z + apart * (1 - 2 * lax.rem(z, 2))
        step = lax.rem(start + N_Z - a // 2, N_Z) // 2
        here = jnp.where(apart == 0, near[step], far[step])
        there = jnp.where(apart == 0, near_twin[step], far_twin[step])
        piece = jnp.where(lax.rem(a, 2) == core, here, there)
        acc[cols[slot]] += lax.dot_general(
            piece, tiles[slot], (((1,), (0,)), ((), ())), preferred_element_type=F32
        )

    out[...] = acc[...].astype(BF16)


def tile_call(kernel, tiles, rows, cols, meta, vectors, out_shape):
    return pl.pallas_call(
        kernel,
        out_shape=out_shape,
        in_specs=[SMEM] * 3 + [VMEM] * (1 + len(vectors)),
        out_specs=jax.tree.map(lambda o: VMEM, out_shape),
        scratch_shapes=[pltpu.VMEM((16, K, BS), F32)],
        compiler_params=PARAMS,
    )(rows, cols, meta, tiles, *vectors)


def cast_kernel(block, out):
    out[...] = block[...].astype(BF16)


def cast(block):
    return pl.pallas_call(
        cast_kernel,
        out_shape=jax.ShapeDtypeStruct((K, BS), BF16),
        in_specs=[VMEM],
        out_specs=VMEM,
        compiler_params=PARAMS,
    )(block)


def collect_kernel(*refs):
    for i in range(N_QUAD):
        refs[N_QUAD][i] = refs[i][...]


def collect(pieces):
    return pl.pallas_call(
        collect_kernel,
        out_shape=jax.ShapeDtypeStruct((N_QUAD, K, BS), BF16),
        in_specs=[VMEM] * N_QUAD,
        out_specs=VMEM,
        compiler_params=PARAMS,
    )(*pieces)


def pass_kernel(mine, other, out):
    out[...] = (mine[N_QUAD:] + other[N_QUAD:]).astype(BF16)


def pass_on(mine, other):
    return pl.pallas_call(
        pass_kernel,
        out_shape=jax.ShapeDtypeStruct((N_QUAD, K, BS), BF16),
        in_specs=[VMEM] * 2,
        out_specs=VMEM,
        compiler_params=PARAMS,
    )(mine, other)


def join_kernel(mine, other, passed, *outs):
    for i in range(N_QUAD):
        total = mine[i] + other[i] + passed[i].astype(F32)
        outs[i][...] = total.astype(outs[i].dtype)


def join(mine, other, passed):
    return pl.pallas_call(
        join_kernel,
        out_shape=[jax.ShapeDtypeStruct((K, BS), F32)]
        + [jax.ShapeDtypeStruct((K, BS), BF16)] * (N_QUAD - 1),
        in_specs=[VMEM] * 3,
        out_specs=[VMEM] * N_QUAD,
        compiler_params=PARAMS,
    )(mine, other, passed)


def product_kernel(n_basis, by_row, *refs):
    pieces = refs[:N_QUAD]
    basis = refs[N_QUAD : N_QUAD + n_basis]
    product_ref, inner_ref = refs[N_QUAD + n_basis :]
    total = by_row[0].astype(F32)
    for i in range(1, N_ROW):
        total = total + by_row[i].astype(F32)
    for piece in pieces:
        total = total + piece[...].astype(F32)
    product_ref[...] = total
    for i in range(n_basis):
        inner_ref[:, i * K : (i + 1) * K] = dot_nt(total, basis[i][...])
    inner_ref[:, n_basis * K : (n_basis + 1) * K] = dot_nt(total, total)


def product_call(by_row, pieces, basis):
    n = len(basis)
    return pl.pallas_call(
        functools.partial(product_kernel, n),
        out_shape=[
            jax.ShapeDtypeStruct((K, BS), F32),
            jax.ShapeDtypeStruct((K, (n + 1) * K), F32),
        ],
        in_specs=[VMEM] * (1 + N_QUAD + n),
        out_specs=[VMEM] * 2,
        compiler_params=PARAMS,
    )(by_row, *pieces, *basis)


def gram_kernel(block, out):
    out[...] = dot_nt(block[...], block[...])


def gram_call(block):
    return pl.pallas_call(
        gram_kernel,
        out_shape=jax.ShapeDtypeStruct((K, K), F32),
        in_specs=[VMEM],
        out_specs=VMEM,
        compiler_params=PARAMS,
    )(block)


def factor(gram):
    row_id = lax.broadcasted_iota(jnp.int32, (K, K), 0)
    col_id = lax.broadcasted_iota(jnp.int32, (K, K), 1)
    unit = (row_id == col_id).astype(F32)
    work = jnp.concatenate([gram, unit], axis=1)
    ids = lax.broadcasted_iota(jnp.int32, (8, 1), 0)
    n = K // 8
    parts = [work[8 * i : 8 * i + 8] for i in range(n)]
    columns = {}

    def take(c):
        columns[c] = {
            i: jnp.broadcast_to(parts[i][:, c : c + 1], (8, 2 * K)) for i in range(c // 8, n)
        }

    for c in range(AHEAD):
        take(c)
    for k in range(K - 1):
        p, o = divmod(k, 8)
        if k + AHEAD < K:
            take(k + AHEAD)
        column = columns.pop(k)
        inverse = 1.0 / column[p][o : o + 1]
        scaled = parts[p][o : o + 1] * inverse
        for c in range(k + 1, min(k + AHEAD + 1, K)):
            q, r = divmod(c, 8)
            factor_c = column[q][r : r + 1] * inverse
            for i in range(q, n):
                columns[c][i] = columns[c][i] - column[i] * factor_c
        for i in range(p, n):
            multiplier = jnp.where(ids > o, column[i], 0.0) if i == p else column[i]
            parts[i] = parts[i] - multiplier * scaled
    work = jnp.concatenate(parts, axis=0)
    scale = jnp.sum(jnp.where(row_id == col_id, work[:, :K], 0.0), axis=1, keepdims=True)
    work = work * (1.0 / jnp.sqrt(scale))
    upper = jnp.where(row_id <= col_id, work[:, :K], 0.0)
    inverse = jnp.where(row_id >= col_id, work[:, K:], 0.0)
    return upper, inverse


def finish_kernel(n_basis, labels, n_records, sums, block_ref, *refs):
    basis = refs[:n_basis]
    records = refs[n_basis : n_basis + n_records]
    outs = refs[n_basis + n_records :]
    inner = sums[...] / labels
    gram = inner[:, n_basis * K : (n_basis + 1) * K]
    residual = block_ref[...]
    for i in range(n_basis):
        coeffs_t = inner[:, i * K : (i + 1) * K]
        gram = gram - dot_nt(coeffs_t, coeffs_t)
        residual = residual - dot_nn(coeffs_t, basis[i][...])
    upper, inverse = factor(gram)
    current = dot_nn(inverse, residual)
    if n_records:
        basis_ref, record_ref = outs
        for i in range(1, n_basis):
            basis_ref[i - 1] = basis[i][...]
        basis_ref[n_basis - 1] = current
        for i in range(n_records):
            record_ref[i] = records[i][...]
        record_ref[n_records, 0] = inner[:, (n_basis - 1) * K : n_basis * K].T
        record_ref[n_records, 1] = upper
        return
    current_ref, spread_ref = outs[:2]
    current_ref[...] = current
    vectors = current.astype(BF16)
    for i in range(N_ROW):
        spread_ref[i] = vectors
    if n_basis:
        outs[2][0] = inner[:, (n_basis - 1) * K : n_basis * K].T
        outs[2][1] = upper


def finish_call(sums, block, basis, labels, records):
    n = len(basis)
    if records:
        out_shape = [
            jax.ShapeDtypeStruct((n, K, BS), F32),
            jax.ShapeDtypeStruct((n, 2, K, K), F32),
        ]
    else:
        out_shape = [
            jax.ShapeDtypeStruct((K, BS), F32),
            jax.ShapeDtypeStruct((N_ROW, K, BS), BF16),
        ]
        if n:
            out_shape.append(jax.ShapeDtypeStruct((2, K, K), F32))
    return pl.pallas_call(
        functools.partial(finish_kernel, n, labels, len(records)),
        out_shape=out_shape,
        in_specs=[VMEM] * (2 + n + len(records)),
        out_specs=[VMEM] * len(out_shape),
        compiler_params=PARAMS,
    )(sums, block, *basis, *records)


def per_device(tile_values, tile_rows, tile_cols, tile_count, start_block):
    tiles = tile_values[0]
    rows, cols = tile_rows[0], tile_cols[0]
    place = [lax.axis_index("core"), lax.axis_index("z")]
    meta = jnp.stack([tile_count[0, 0]] + place).astype(jnp.int32)
    labels = float(BS * N_ROW * N_COL)

    sums = all_sum(gram_call(start_block))
    current, spread = finish_call(sums, start_block, [], labels, [])
    basis = [current]
    records = []
    for iteration in range(ITERS):
        col_vectors = lax.all_to_all(spread, ROW, 0, 0, tiled=True)
        vectors = cast(basis[-1])
        near = collect([vectors] + [permute(vectors, "z", z_pairs(s)) for s in range(1, N_QUAD)])
        far = permute(near, "z", NEXT_Z)
        near_twin = permute(near, "core", TWIN)
        far_twin = permute(far, "core", TWIN)
        half = jax.ShapeDtypeStruct((N_Z, K, BS), F32)
        mine, other = tile_call(forward_kernel, tiles, rows, cols, meta, [col_vectors, near_twin], [half, half])
        other = permute(other, "core", TWIN)
        part_col = tile_call(
            backward_kernel, tiles, rows, cols, meta, [near, far, near_twin, far_twin],
            jax.ShapeDtypeStruct((N_ROW, K, BS), BF16),
        )
        by_row = lax.all_to_all(part_col, ROW, 0, 0, tiled=True)
        passed = permute(pass_on(mine, other), "z", NEXT_Z)
        pieces = join(mine, other, passed)
        pieces = [pieces[0]] + [permute(pieces[s], "z", z_pairs(s)) for s in range(1, N_QUAD)]
        product, inner = product_call(by_row, pieces, basis)
        sums = all_sum(inner)
        last = iteration == ITERS - 1
        result = finish_call(sums, product, basis, labels, records if last else [])
        if last:
            return tuple(result)
        current, spread, record = result
        basis.append(current)
        records.append(record)


def solution(mesh):
    devices = mesh.devices.reshape(4, 4, N_Z, 2)
    fine = jax.sharding.Mesh(devices, ROW + COL)
    in_specs = (
        P(ROW, COL, None, None),
        P(ROW, COL),
        P(ROW, COL),
        P(ROW, COL),
        P(None, ROW + COL),
    )
    out_specs = (P(None, None, ROW + COL), P())
    return jax.shard_map(
        per_device, mesh=fine, in_specs=in_specs, out_specs=out_specs, check_vma=False
    )
```
